128 devices in a mesh: dp: 16 (over x, y_lo, core), tensor: 8 (over z, y_hi).
Axes of the slice: x: 4, y: 4 (y_hi: 2, y_lo: 2; y = y_hi * 2 + y_lo), z: 4, core: 2. Of those that a mesh axis runs over, the one named last changes fastest.
Arguments:
- acts: bfloat16 [128, 64, 4096], P('dp'), may hold values from -6 to 6
- output_gradient: bfloat16 [128, 64, 4096], P('dp', None, 'tensor'), may hold values from -6 to 6
- adapter_down_matrix: bfloat16 [64, 4096], replicated, may hold values from -0.09375 to 0.09375
- adapter_up_matrix: bfloat16 [4096, 64], P('tensor'), may hold values from -0.09375 to 0.09375
- counts: int32 [128], P('dp'), may hold values from 8 to 64, as said below
- signs: int32 [8, 512, 128, 1024], P('tensor', 'dp'), may hold values from 0 to 255
- bank: bfloat16 [128, 8192], replicated, may hold values from -6 to 6
- validation_rows: int32 [64], replicated, may hold values from 0 to 127
Outputs:
- features: float32 [128, 8192], P(('dp', 'tensor'))
- scores: float32 [128, 64], P(('dp', 'tensor'))
The draws below stay inside these ranges and needn't reach their ends.
Inputs may be any that keep to these rules, and one draw needn't show every extreme that they name: Tokens at positions below counts are real; at least one example has all 64 tokens real. Each word carries 8 independent signs in its low 8 bits.
All inputs are finite; a program needn't handle non-finite values.
Results may differ from the reference program's by a relative error of at most 0.0042.
Values may be sent and summed in bfloat16 or wider, within the bound.
A program may use at most 128 MiB of HBM per device.

```python
import math
import jax
import jax.numpy as jnp
from jax import lax

MODEL_WIDTH = 4096
ADAPTER_RANK = 64
PROJ = 8192
SEQ = 64
BANK = 128
NVAL = 64
EXAMPLES = 128
N_TENSOR = 8


def draw_counts(key, part):
    key = jax.random.fold_in(key, 7)
    first_key, second_key = jax.random.split(key)
    lengths = jax.random.randint(first_key, (EXAMPLES,), SEQ // 8, SEQ + 1, dtype=jnp.int32)
    filled = jax.random.randint(second_key, (), 0, EXAMPLES, dtype=jnp.int32)
    return lengths.at[filled].set(SEQ)


def touch_ends(array, own_key, least, top_value):
    longest = array.shape.index(max(array.shape))
    spots = []
    for shift in (0, 1):
        where = [jax.random.randint(jax.random.fold_in(own_key, axis), (), 0, length) for axis, length in enumerate(array.shape)]
        where[longest] = (where[longest] + shift) % array.shape[longest]
        spots.append(tuple(where))
    return array.at[spots[0]].set(least).at[spots[1]].set(top_value)


def block_scale(rng, extent, cuts, least, top_value):
    gain = 1.0
    for axis_at, shards_of in cuts:
        steps = jax.random.uniform(jax.random.fold_in(jax.random.fold_in(rng, 6), axis_at), (shards_of,), jnp.float32, least / len(cuts), top_value / len(cuts))
        gain = gain * jnp.repeat(jnp.exp(steps), extent[axis_at] // shards_of).reshape((-1,) + (1,) * (len(extent) - 1 - axis_at))
    return gain


def centred(own_key, extent, scale, reach, shards=(), kind=jnp.bfloat16):
    drawn = scale * jax.random.normal(own_key, extent, jnp.float32)
    if shards:
        drawn = drawn * block_scale(own_key, extent, shards, -0.22, 0.18)
    return jnp.clip(drawn, -reach, reach).astype(kind)


def setup_inputs(seed: int = 0) -> dict:
    keys = jax.random.split(jax.random.key(seed), 9)
    acts = centred(keys[0], (EXAMPLES, SEQ, MODEL_WIDTH), 1.0, 6.0, ((0, 16),))
    output_gradient = centred(keys[1], (EXAMPLES, SEQ, MODEL_WIDTH), 1.0, 6.0, ((0, 16), (2, 8)))
    adapter_down_matrix = centred(keys[2], (ADAPTER_RANK, MODEL_WIDTH), MODEL_WIDTH ** -0.5, 0.09375)
    adapter_up_matrix = centred(keys[3], (MODEL_WIDTH, ADAPTER_RANK), MODEL_WIDTH ** -0.5, 0.09375, ((0, 8),))
    counts = draw_counts(jax.random.fold_in(keys[8], 71), 0)
    signs = touch_ends(jax.random.randint(keys[5], (N_TENSOR, MODEL_WIDTH // N_TENSOR, 2 * ADAPTER_RANK, PROJ // 8), 0, 256), jax.random.fold_in(keys[5], 1), 0, 255).astype(jnp.int32)
    bank = centred(keys[6], (BANK, PROJ), 1.0, 6.0)
    validation_rows = touch_ends(jax.random.randint(keys[7], (NVAL,), 0, BANK), jax.random.fold_in(keys[7], 1), 0, BANK - 1).astype(jnp.int32)
    return dict(acts=acts, output_gradient=output_gradient, adapter_down_matrix=adapter_down_matrix, adapter_up_matrix=adapter_up_matrix, counts=counts, signs=signs, bank=bank, validation_rows=validation_rows)


def unpack_signs(packed_words):
    shifts = jnp.arange(8, dtype=jnp.int32)
    bit_vals = jnp.bitwise_and(jnp.right_shift(packed_words[..., None, :], shifts[:, None]), 1)
    new_shape = packed_words.shape[:-1] + (8 * packed_words.shape[-1],)
    return (2 * bit_vals - 1).astype(jnp.bfloat16).reshape(new_shape)

def reference(acts, output_gradient, adapter_down_matrix, adapter_up_matrix, counts, signs, bank, validation_rows):
    examples = acts.shape[0]
    positions = jnp.arange(SEQ, dtype=jnp.int32)
    keep_mask = positions[None, :] < counts[:, None]
    masked_output = jnp.where(keep_mask[:, :, None], output_gradient, jnp.zeros_like(output_gradient))
    hidden_state = jnp.dot(acts.reshape(-1, MODEL_WIDTH), adapter_down_matrix.T, preferred_element_type=jnp.float32).astype(jnp.bfloat16)
    coupled_gradient = jnp.dot(masked_output.reshape(-1, MODEL_WIDTH), adapter_up_matrix, preferred_element_type=jnp.float32).astype(jnp.bfloat16)
    hidden_state = lax.optimization_barrier(hidden_state).astype(jnp.float32).reshape(examples, SEQ, ADAPTER_RANK)
    coupled_gradient = lax.optimization_barrier(coupled_gradient).astype(jnp.float32).reshape(examples, SEQ, ADAPTER_RANK)
    grad_a = jnp.einsum('esj,esr->jer', acts.astype(jnp.float32), coupled_gradient, precision=lax.Precision.HIGHEST)
    grad_b = jnp.einsum('esj,esr->jer', masked_output.astype(jnp.float32), hidden_state, precision=lax.Precision.HIGHEST)
    gradient = jnp.concatenate([grad_a, grad_b], axis=2).astype(jnp.bfloat16)
    sign_words = signs.reshape(MODEL_WIDTH, 2 * ADAPTER_RANK, PROJ // 8)
    block_rows = math.gcd(MODEL_WIDTH, 32)
    grad_blocks = gradient.reshape(MODEL_WIDTH // block_rows, block_rows, examples, 2 * ADAPTER_RANK)
    word_blocks = sign_words.reshape(MODEL_WIDTH // block_rows, block_rows, 2 * ADAPTER_RANK, PROJ // 8)

    def accumulate(totals, pieces):
        grad_block, word_block = pieces
        sign_block = unpack_signs(word_block).reshape(block_rows * 2 * ADAPTER_RANK, PROJ)
        flat_grad = jnp.transpose(grad_block, (1, 0, 2)).reshape(examples, block_rows * 2 * ADAPTER_RANK)
        return (totals + jnp.dot(flat_grad, sign_block, preferred_element_type=jnp.float32), None)
    projected, _ = lax.scan(accumulate, jnp.zeros((examples, PROJ), jnp.float32), (grad_blocks, word_blocks))
    mean_sq = lax.optimization_barrier(jnp.mean(projected * projected, axis=1, keepdims=True))
    features = projected * lax.rsqrt(mean_sq + 1e-06)
    chosen = bank[validation_rows].astype(jnp.float32)
    scores = jnp.dot(features, chosen.T, precision=lax.Precision.HIGHEST) / math.sqrt(PROJ)
    return (features, scores)
```

```python
import math

import jax
import jax.numpy as jnp
from jax import lax
from jax.experimental import pallas as pl
from jax.experimental.pallas import tpu as pltpu
from jax.sharding import PartitionSpec as P

BF16 = jnp.bfloat16
F32 = jnp.float32
MESH = pl.DeviceIdType.MESH

NDP = 16
NT = 8
EPD = 8
SEQ = 64
RANK = 64
WIDTH = 4096
SLICE = 512
ROWS = 32
WORDS = 1024
NS = 4
SW = WORDS // NS
HALFK = ROWS * RANK
AXES = ("x", "z", "x", "z")


def dot(a, b, dims=(((1,), (0,)), ((), ()))):
    return lax.dot_general(a, b, dims, preferred_element_type=F32)


def body(
    acts_hbm, og_hbm, down_hbm, up_hbm, counts, signs_hbm, bank_hbm, vrows_hbm,
    feat_out, score_out,
    acts, mg, down2, up, bank, vrows, words, nib,
    pu, pu_recv, cpl_recv, cpl4, hid4,
    sb, rb, trans, grad, acc, rowsum,
    part, s0, r0, s1, r1, k1, s2, r2, feat,
    in_sem, word_sem, own_sem, snd, rcv,
):
    d = lax.axis_index("dp")
    t = lax.axis_index("tensor")
    x = d // 4
    y_lo = (d // 2) % 2
    core = d % 2
    z = t // 2
    y_hi = t % 2

    def load(src, dst, n):
        c = pltpu.make_async_copy(src, dst, in_sem.at[n])
        c.start()
        return c

    c_og = load(og_hbm, mg, 0)
    c_up = load(up_hbm, up, 1)
    c_down = [load(down_hbm, down2.at[pl.ds(i * RANK, RANK)], 2 + i) for i in range(2)]
    c_acts = [
        load(acts_hbm.at[pl.ds(i * 128, 128)], acts.at[pl.ds(i * 128, 128)], 4 + i) for i in range(4)
    ]
    c_words = []
    for i in range(8):
        c = pltpu.make_async_copy(
            signs_hbm.at[pl.ds(i * 4, 4)], words.at[pl.ds(i * 4, 4)], word_sem.at[i]
        )
        c.start()
        c_words.append(c)
    c_bank = load(bank_hbm, bank, 8)
    c_vrows = load(vrows_hbm, vrows, 9)

    barrier = pltpu.get_barrier_semaphore()

    def greet(dd, tt):
        pl.semaphore_signal(
            barrier, inc=1, device_id={"dp": dd, "tensor": tt}, device_id_type=MESH
        )

    for k in range(1, NDP):
        greet((d + k) % NDP, t)
    for k in range(1, NT):
        greet(d, (t + k) % NT)
    d_flip = d + 2 - 4 * y_lo
    t_flip = t + 1 - 2 * y_hi
    for k in range(1, NT):
        greet(d_flip, (t + k) % NT)
    for k in range(1, 8):
        m = (x * 2 + y_lo + k) % 8
        greet(m * 2 + core, t_flip)

    lane = lax.broadcasted_iota(jnp.int32, (1, 128), 1)
    low = lane < 64

    def split4(v):
        zero = jnp.zeros_like(v)
        return jnp.concatenate([jnp.where(low, v, zero), jnp.where(low, zero, v)], axis=1)

    c_og.wait()
    token = lax.broadcasted_iota(jnp.int32, (SEQ, SLICE), 0)
    for e in range(EPD):
        rows = pl.ds(e * SEQ, SEQ)
        v = mg[rows, :].astype(F32)
        mg[rows, :] = jnp.where(token < counts[e], v, 0.0).astype(BF16)

    c_up.wait()
    eye2 = (
        lax.broadcasted_iota(jnp.int32, (RANK, 128), 1) % RANK
        == lax.broadcasted_iota(jnp.int32, (RANK, 128), 0)
    ).astype(F32).astype(BF16)
    up4 = split4(dot(up[...], eye2)).astype(BF16)
    pu[...] = (
        dot(mg[0:256, :], up4[:, 0:128]) + dot(mg[256:512, :], up4[:, 128:256])
    )

    pl.semaphore_wait(barrier, 36)

    def send_pu(k, _):
        tt = (t + k) % NT
        pltpu.make_async_remote_copy(
            src_ref=pu.at[pl.ds(pl.multiple_of(tt * 32, 32), 32)],
            dst_ref=pu_recv.at[k - 1],
            send_sem=snd.at[0],
            recv_sem=rcv.at[0],
            device_id={"dp": d, "tensor": tt},
            device_id_type=MESH,
        ).start()
        return 0

    lax.fori_loop(1, NT, send_pu, 0)

    for c in c_down:
        c.wait()
    for i in range(4):
        c_acts[i].wait()
        rows = pl.ds(i * 128, 128)
        h = dot(acts[rows, :], down2[...], (((1,), (1,)), ((), ())))
        hid4[rows, :] = split4(h).astype(BF16)

    def outer(lhs, rhs, half):
        def one(e, _):
            rows = pl.ds(pl.multiple_of(e * SEQ, SEQ), SEQ)
            o = dot(lhs(rows), rhs[rows, :], (((0,), (0,)), ((), ())))
            o = o.reshape(NDP, 2, 16, 256)
            g = o[:, 0, :, 0:128] + o[:, 1, :, 128:256]
            sb[half, :, e] = g.astype(BF16)
            return 0

        lax.fori_loop(0, EPD, one, 0)

    def send_grad(half):
        def one(k, _):
            dd = (d + k) % NDP
            pltpu.make_async_remote_copy(
                src_ref=sb.at[half, dd],
                dst_ref=rb.at[half, d],
                send_sem=snd.at[2 + half],
                recv_sem=rcv.at[2 + half],
                device_id={"dp": dd, "tensor": t},
                device_id_type=MESH,
            ).start()
            return 0

        lax.fori_loop(1, NDP, one, 0)
        own = pltpu.make_async_copy(sb.at[half, d], rb.at[half, d], own_sem.at[half])
        own.start()
        return own

    def wait_bytes(ref, sem):
        pltpu.make_async_copy(ref, ref, sem).wait()

    outer(lambda rows: mg[rows, :], hid4, 1)
    own_b = send_grad(1)

    wait_bytes(pu_recv, rcv.at[0])
    total = pu[pl.ds(pl.multiple_of(t * 32, 32), 32), :]
    for k in range(NT - 1):
        total = total + pu_recv[k]
    cpl_recv[t] = total.astype(BF16)

    def send_cpl(k, _):
        tt = (t + k) % NT
        pltpu.make_async_remote_copy(
            src_ref=cpl_recv.at[t],
            dst_ref=cpl_recv.at[t],
            send_sem=snd.at[1],
            recv_sem=rcv.at[1],
            device_id={"dp": d, "tensor": tt},
            device_id_type=MESH,
        ).start()
        return 0

    lax.fori_loop(1, NT, send_cpl, 0)

    def convert(half, hi):
        def one(jp, _):
            w = words[jp + 16 * hi, pl.ds(half * RANK, RANK), :]
            rows = pl.ds(hi * RANK, RANK)
            quarter = jnp.asarray(0.25, BF16)
            nib[0, half, jp, rows, :] = (w & 15).astype(F32).astype(BF16) + quarter
            nib[1, half, jp, rows, :] = (w >> 4).astype(F32).astype(BF16) + quarter
            return 0

        lax.fori_loop(0, 16, one, 0)

    for c in c_words:
        c.wait()
    convert(1, 0)

    wait_bytes(cpl_recv.at[pl.ds(0, NT - 1)], rcv.at[1])
    v = cpl_recv[...].reshape(256, 128).astype(F32)
    w = pltpu.roll(v, 64, 1)
    zero = jnp.zeros_like(v)
    cpl4[0:256, 0:128] = jnp.where(low, v, zero).astype(BF16)
    cpl4[0:256, 128:256] = jnp.where(low, zero, w).astype(BF16)
    cpl4[256:512, 0:128] = jnp.where(low, w, zero).astype(BF16)
    cpl4[256:512, 128:256] = jnp.where(low, zero, v).astype(BF16)
    offset = pl.multiple_of(t * SLICE, SLICE)
    outer(lambda rows: acts[rows, pl.ds(offset, SLICE)], cpl4, 0)
    own_a = send_grad(0)

    convert(1, 1)
    convert(0, 0)
    convert(0, 1)

    ones = jnp.ones((HALFK, 128), BF16)

    def gather(half, own):
        own.wait()
        wait_bytes(rb.at[half, pl.ds(0, NDP - 1)], rcv.at[2 + half])
        trans[...] = rb[half].reshape(2048, 128).astype(F32)
        for jp in range(16):
            grad[half, :, jp * 128:(jp + 1) * 128] = trans[
                pl.ds(jp, 128, stride=16), :
            ].astype(BF16)

    def planes(half, s):
        g = grad[half]
        cols = pl.ds(s * SW, SW) if isinstance(s, int) else pl.ds(pl.multiple_of(s * SW, SW), SW)
        out = []
        for q in range(2):
            n = nib[q, half, :, :, cols].reshape(HALFK, SW)
            res = [dot(g, n)]
            for k in (4, 3, 2):
                shift = jnp.asarray(2.0 ** (7 + k), BF16)
                res.append(dot(g, (n + shift) - shift))
            out.append(res)
        return out

    gather(1, own_b)
    rowsum[...] = dot(grad[1], ones)

    def first(s, _):
        got = planes(1, s)
        for q in range(2):
            for i in range(4):
                acc[s, q, i] = got[q][i]
        return 0

    lax.fori_loop(0, NS, first, 0)

    gather(0, own_a)
    rowsum[...] += dot(grad[0], ones)

    def compute(s):
        got = planes(0, s)
        r = rowsum[...]
        for h in range(SW // 128):
            cols = slice(h * 128, (h + 1) * 128)
            for q in range(2):
                d0, d4, d3, d2 = (got[q][i][:, cols] + acc[s, q, i, :, cols] for i in range(4))
                a4, a3 = d4 * 0.125, d3 * 0.25
                p3 = a4 - r
                p2 = a3 - a4 - r
                p1 = d2 * 0.5 - a3 - a4 - r
                p0 = 2.0 * d0 - d2 - 2.0 * a3 - 2.0 * a4 - 1.5 * r
                for i, p in enumerate((p0, p1, p2, p3)):
                    row = h * 8 + q * 4 + i
                    for dd in range(NDP):
                        v = p[dd * 8:(dd + 1) * 8, :]
                        if AXES[s] == "x":
                            base = (dd % 2) * 64 + (dd // 2) * 8
                            where = pl.ds(base * 16 + row, 8, stride=16)
                        else:
                            base = (dd % 2) * 64 + dd // 2
                            where = pl.ds(base * 16 + row, 8, stride=128)
                        part[s, where, :] = v
        theirs = pl.ds(pl.multiple_of((1 - core) * 1024, 1024), 1024)
        s0[s] = part[s, theirs, :].astype(BF16)
        pltpu.make_async_remote_copy(
            src_ref=s0.at[s],
            dst_ref=r0.at[s],
            send_sem=snd.at[4 + 3 * s],
            recv_sem=rcv.at[4 + 3 * s],
            device_id={"dp": d + 1 - 2 * core, "tensor": t},
            device_id_type=MESH,
        ).start()

    def along(s):
        wait_bytes(r0.at[s], rcv.at[4 + 3 * s])
        a = x if AXES[s] == "x" else z
        for k in (1, 2, 3, 0):
            g = (a + k) % 4
            mine = pl.ds(pl.multiple_of(core * 1024 + g * 256, 256), 256)
            v = part[s, mine, :] + r0[s, pl.ds(pl.multiple_of(g * 256, 256), 256), :].astype(F32)
            if k == 0:
                k1[s] = v
                continue
            s1[s, k - 1] = v.astype(BF16)
            if AXES[s] == "x":
                peer = {"dp": g * 4 + d % 4, "tensor": t}
            else:
                peer = {"dp": d, "tensor": g * 2 + y_hi}
            pltpu.make_async_remote_copy(
                src_ref=s1.at[s, k - 1],
                dst_ref=r1.at[s, k - 1],
                send_sem=snd.at[5 + 3 * s],
                recv_sem=rcv.at[5 + 3 * s],
                device_id=peer,
                device_id_type=MESH,
            ).start()

    def place(s):
        if AXES[s] == "x":
            return y_lo * 8 + t
        return y_hi * 8 + x * 2 + y_lo

    def across(s):
        wait_bytes(r1.at[s], rcv.at[5 + 3 * s])
        v = k1[s]
        for k in range(3):
            v = v + r1[s, k].astype(F32)
        s2[s] = v.reshape(16, 16, 128)
        m = place(s)

        def one(k, _):
            mm = (m + k) % 16
            if AXES[s] == "x":
                peer = {"dp": x * 4 + (mm // 8) * 2 + core, "tensor": mm % 8}
            else:
                peer = {"dp": (mm % 8) * 2 + core, "tensor": z * 2 + mm // 8}
            pltpu.make_async_remote_copy(
                src_ref=s2.at[s, mm],
                dst_ref=r2.at[s, k - 1],
                send_sem=snd.at[6 + 3 * s],
                recv_sem=rcv.at[6 + 3 * s],
                device_id=peer,
                device_id_type=MESH,
            ).start()
            return 0

        lax.fori_loop(1, 16, one, 0)

    def owned(s, score):
        wait_bytes(r2.at[s], rcv.at[6 + 3 * s])
        v = s2[s, place(s)]
        for k in range(15):
            v = v + r2[s, k]
        for h in range(2):
            feat[pl.ds(s * 2 + h, 8, stride=8), :] = v[h * 8:(h + 1) * 8, :]
            for b in range(8):
                cols = b * WORDS + s * SW + h * 128
                score = score + v[h * 8 + b:h * 8 + b + 1, :] * bank[:, cols:cols + 128].astype(F32)
        return score

    compute(0)
    compute(1)
    along(0)
    compute(2)
    along(1)
    compute(3)
    along(2)
    across(0)
    along(3)
    across(1)
    across(2)
    c_bank.wait()
    c_vrows.wait()
    score = jnp.zeros((128, 128), F32)
    score = owned(0, score)
    score = owned(1, score)
    across(3)
    score = owned(2, score)
    score = owned(3, score)

    f = feat[...]
    mean = jnp.sum(f * f, keepdims=True) * (1.0 / (8 * WORDS))
    inv = lax.rsqrt(mean + 1e-06)
    feat_out[...] = f * inv
    by_row = jnp.sum(score, axis=1, keepdims=True)
    pick = lax.broadcasted_iota(jnp.int32, (128, 64), 0) == vrows[...]
    chosen = jnp.sum(jnp.where(pick, by_row, 0.0), axis=0, keepdims=True)
    score_out[...] = chosen * inv * (1.0 / math.sqrt(8 * WORDS))

    wait_bytes(pu_recv, snd.at[0])
    wait_bytes(cpl_recv.at[pl.ds(0, NT - 1)], snd.at[1])
    for half in range(2):
        wait_bytes(sb.at[half, pl.ds(0, NDP - 1)], snd.at[2 + half])
    for s in range(NS):
        wait_bytes(s0.at[s], snd.at[4 + 3 * s])
        wait_bytes(s1.at[s], snd.at[5 + 3 * s])
        wait_bytes(s2.at[s, pl.ds(0, 15)], snd.at[6 + 3 * s])


def per_device(acts, og, down, up, counts, signs, bank, vrows):
    anywhere = pl.BlockSpec(memory_space=pl.ANY)
    vmem = pltpu.VMEM
    feat, score = pl.pallas_call(
        body,
        out_shape=(
            jax.ShapeDtypeStruct((64, 128), F32),
            jax.ShapeDtypeStruct((1, 64), F32),
        ),
        in_specs=[
            anywhere, anywhere, anywhere, anywhere,
            pl.BlockSpec(memory_space=pltpu.SMEM),
            anywhere, anywhere, anywhere,
        ],
        out_specs=(pl.BlockSpec(memory_space=pltpu.VMEM),) * 2,
        scratch_shapes=[
            vmem((EPD * SEQ, WIDTH), BF16),
            vmem((EPD * SEQ, SLICE), BF16),
            vmem((2 * RANK, WIDTH), BF16),
            vmem((SLICE, RANK), BF16),
            vmem((128, 8 * WORDS), BF16),
            vmem((1, 64), jnp.int32),
            vmem((ROWS, 128, WORDS), jnp.int32),
            vmem((2, 2, 16, 128, WORDS), BF16),
            vmem((256, 128), F32),
            vmem((NT - 1, 32, 128), F32),
            vmem((NT, 32, 128), BF16),
            vmem((EPD * SEQ, 256), BF16),
            vmem((EPD * SEQ, 256), BF16),
            vmem((2, NDP, EPD, 16, 128), BF16),
            vmem((2, NDP, EPD, 16, 128), BF16),
            vmem((2048, 128), F32),
            vmem((2, 128, HALFK), BF16),
            vmem((NS, 2, 4, 128, SW), F32),
            vmem((128, 128), F32),
            vmem((NS, 2048, 128), F32),
            vmem((NS, 1024, 128), BF16),
            vmem((NS, 1024, 128), BF16),
            vmem((NS, 3, 256, 128), BF16),
            vmem((NS, 3, 256, 128), BF16),
            vmem((NS, 256, 128), F32),
            vmem((NS, 16, 16, 128), F32),
            vmem((NS, 15, 16, 128), F32),
            vmem((64, 128), F32),
            pltpu.SemaphoreType.DMA((10,)),
            pltpu.SemaphoreType.DMA((8,)),
            pltpu.SemaphoreType.DMA((2,)),
            pltpu.SemaphoreType.DMA((4 + 3 * NS,)),
            pltpu.SemaphoreType.DMA((4 + 3 * NS,)),
        ],
        compiler_params=pltpu.CompilerParams(
            collective_id=0, has_side_effects=True, vmem_limit_bytes=63 << 20
        ),
    )(
        acts.reshape(EPD * SEQ, WIDTH),
        og.reshape(EPD * SEQ, SLICE),
        down,
        up,
        counts,
        signs.reshape(ROWS, 128, WORDS),
        bank,
        vrows.reshape(1, 64),
    )
    return feat.reshape(1, 8 * WORDS), score


def solution(mesh):
    in_specs = (
        P("dp", None, None),
        P("dp", None, "tensor"),
        P(),
        P("tensor", None),
        P("dp"),
        P("tensor", "dp", None, None),
        P(),
        P(),
    )
    out_specs = (P(("dp", "tensor"), None), P(("dp", "tensor"), None))
    return jax.shard_map(
        per_device, mesh=mesh, in_specs=in_specs, out_specs=out_specs, check_vma=False
    )
```

```python
import math

import jax
import jax.numpy as jnp
from jax import lax
from jax.experimental import pallas as pl
from jax.experimental.pallas import tpu as pltpu
from jax.sharding import PartitionSpec as P

BF16 = jnp.bfloat16
F32 = jnp.float32
MESH = pl.DeviceIdType.MESH

NDP = 16
NT = 8
EPD = 8
SEQ = 64
RANK = 64
WIDTH = 4096
SLICE = 512
ROWS = 32
WORDS = 1024
CHUNK = 1024
PARTS = ((1, 0), (1, 1), (0, 0), (0, 1))
AXES = ("x", "z", "y", "x", "z")
WIDTHS = (256, 256, 256, 128, 128)
NS = len(AXES)
STARTS = tuple(sum(WIDTHS[:s]) for s in range(NS))
PER = tuple(w // 16 for w in WIDTHS)
BEFORE = tuple(w // 16 for w in STARTS)


def dot(a, b, dims=(((1,), (0,)), ((), ()))):
    return lax.dot_general(a, b, dims, preferred_element_type=F32)


def body(
    acts_hbm, og_hbm, down_hbm, up_hbm, counts, signs_hbm, bank_hbm, vrows_hbm,
    out,
    acts, mg, down2, up2, bank, vrows, words, nib,
    pu, pu_recv, cpl_recv, cpl4, hid4,
    sb, rb, trans, grad, acc, rowsum,
    part, s0, r0, s1, r1, k1, s2b, r2b, s2f, r2f, feat,
    in_sem, word_sem, own_sem, snd, rcv,
):
    d = lax.axis_index("dp")
    t = lax.axis_index("tensor")
    x = d // 4
    y_lo = (d // 2) % 2
    core = d % 2
    z = t // 2
    y_hi = t % 2

    def load(src, dst, n):
        c = pltpu.make_async_copy(src, dst, in_sem.at[n])
        c.start()
        return c

    c_og = load(og_hbm, mg, 0)
    c_up = [load(up_hbm, up2.at[pl.ds(i * RANK, RANK)], 10 + i) for i in range(2)]
    c_down = [load(down_hbm, down2.at[pl.ds(i * RANK, RANK)], 2 + i) for i in range(2)]
    for i in range(4):
        load(acts_hbm.at[pl.ds(i * 128, 128)], acts.at[pl.ds(i * 128, 128)], 4 + i)

    barrier = pltpu.get_barrier_semaphore()

    def greet(dd, tt):
        pl.semaphore_signal(
            barrier, inc=1, device_id={"dp": dd, "tensor": tt}, device_id_type=MESH
        )

    for k in range(1, NDP):
        greet((d + k) % NDP, t)
    for k in range(1, NT):
        greet(d, (t + k) % NT)
    d_flip = d + 2 - 4 * y_lo
    t_flip = t + 1 - 2 * y_hi
    for k in range(1, NT):
        greet(d_flip, (t + k) % NT)
    for k in range(1, 8):
        m = (x * 2 + y_lo + k) % 8
        greet(m * 2 + core, t_flip)
    for k in range(1, 4):
        for i in range(1, 4):
            greet((d + 4 * k) % NDP, (t + 2 * i) % NT)

    lane = lax.broadcasted_iota(jnp.int32, (1, 128), 1)
    low = lane < 64

    def split4(v):
        zero = jnp.zeros_like(v)
        return jnp.concatenate([jnp.where(low, v, zero), jnp.where(low, zero, v)], axis=1)

    c_og.wait()
    token = lax.broadcasted_iota(jnp.int32, (SEQ, SLICE), 0)
    for e in range(EPD):
        rows = pl.ds(e * SEQ, SEQ)
        v = mg[rows, :].astype(F32)
        mg[rows, :] = jnp.where(token < counts[e], v, 0.0).astype(BF16)

    for c in c_up:
        c.wait()
    u = dot(mg[...], up2[...], (((1,), (1,)), ((), ())))
    pu[...] = jnp.where(low, u[0:256, :], u[256:512, :])

    pl.semaphore_wait(barrier, 45)

    def send_pu(k, _):
        tt = (t + k) % NT
        pltpu.make_async_remote_copy(
            src_ref=pu.at[pl.ds(pl.multiple_of(tt * 32, 32), 32)],
            dst_ref=pu_recv.at[k - 1],
            send_sem=snd.at[0],
            recv_sem=rcv.at[0],
            device_id={"dp": d, "tensor": tt},
            device_id_type=MESH,
        ).start()
        return 0

    lax.fori_loop(1, NT, send_pu, 0)

    for c in c_down:
        c.wait()
    def hidden(i, _):
        rows = pl.ds(pl.multiple_of(i * 128, 128), 128)
        pltpu.make_async_copy(acts_hbm.at[rows], acts.at[rows], in_sem.at[4 + i]).wait()
        h = dot(acts[rows, :], down2[...], (((1,), (1,)), ((), ())))
        hid4[rows, :] = split4(h).astype(BF16)
        return 0

    lax.fori_loop(0, 2, hidden, 0)
    c_words = []
    for n, (half, c) in enumerate(PARTS):
        for hi in range(2):
            at = pl.ds(16 * hi + 8 * c, 8), pl.ds(half * RANK, RANK)
            copy = pltpu.make_async_copy(signs_hbm.at[at], words.at[at], word_sem.at[2 * n + hi])
            copy.start()
            c_words.append(copy)
    c_bank = load(bank_hbm, bank, 8)
    c_vrows = load(vrows_hbm, vrows, 9)
    acc[...] = jnp.zeros_like(acc)
    rowsum[...] = jnp.zeros_like(rowsum)
    lax.fori_loop(2, 4, hidden, 0)

    def outer(lhs, rhs, half):
        def product(e):
            rows = pl.ds(pl.multiple_of(e * SEQ, SEQ), SEQ)
            o = dot(lhs(rows), rhs[rows, :], (((0,), (0,)), ((), ())))
            o = o.reshape(NDP, 2, 16, 256)
            return o[:, 0, :, 0:128] + o[:, 1, :, 128:256]

        def one(p, _):
            g0, g1 = product(2 * p), product(2 * p + 1)
            for c in range(2):
                g = jnp.concatenate([g0[:, c * 8:c * 8 + 8], g1[:, c * 8:c * 8 + 8]], axis=1)
                sb[2 * (1 - half) + c, :, pl.ds(pl.multiple_of(p * 16, 16), 16), :] = g.astype(BF16)
            return 0

        lax.fori_loop(0, EPD // 2, one, 0, unroll=True)

    def send_grad(n):
        def one(k, _):
            dd = (d + k) % NDP
            pltpu.make_async_remote_copy(
                src_ref=sb.at[n, dd],
                dst_ref=rb.at[n, d],
                send_sem=snd.at[2 + n],
                recv_sem=rcv.at[2 + n],
                device_id={"dp": dd, "tensor": t},
                device_id_type=MESH,
            ).start()
            return 0

        lax.fori_loop(1, NDP, one, 0)
        pltpu.make_async_copy(sb.at[n, d], rb.at[n, d], own_sem.at[n]).start()

    def wait_bytes(ref, sem):
        pltpu.make_async_copy(ref, ref, sem).wait()

    outer(lambda rows: mg[rows, :], hid4, 1)

    wait_bytes(pu_recv, rcv.at[0])
    total = pu[pl.ds(pl.multiple_of(t * 32, 32), 32), :]
    for k in range(NT - 1):
        total = total + pu_recv[k]
    cpl_recv[t] = total.astype(BF16)

    def send_cpl(k, _):
        tt = (t + k) % NT
        pltpu.make_async_remote_copy(
            src_ref=cpl_recv.at[t],
            dst_ref=cpl_recv.at[t],
            send_sem=snd.at[1],
            recv_sem=rcv.at[1],
            device_id={"dp": d, "tensor": tt},
            device_id_type=MESH,
        ).start()
        return 0

    lax.fori_loop(1, NT, send_cpl, 0)
    send_grad(0)
    send_grad(1)

    def convert(n):
        half, c = PARTS[n]
        quarter = jnp.asarray(0.25, BF16)
        for hi in range(2):
            c_words[2 * n + hi].wait()

            def one(k, _):
                w = words[8 * c + k + 16 * hi, pl.ds(half * RANK, RANK), :]
                rows = pl.ds(hi * RANK, RANK)
                nib[n, 0, k, rows, :] = (w & 15).astype(F32).astype(BF16) + quarter
                nib[n, 1, k, rows, :] = (w >> 4).astype(F32).astype(BF16) + quarter
                return 0

            lax.fori_loop(0, 8, one, 0)

    convert(0)
    convert(1)

    wait_bytes(cpl_recv.at[pl.ds(0, NT - 1)], rcv.at[1])
    v = cpl_recv[...].reshape(256, 128).astype(F32)
    w = pltpu.roll(v, 64, 1)
    zero = jnp.zeros_like(v)
    cpl4[0:256, 0:128] = jnp.where(low, v, zero).astype(BF16)
    cpl4[0:256, 128:256] = jnp.where(low, zero, w).astype(BF16)
    cpl4[256:512, 0:128] = jnp.where(low, w, zero).astype(BF16)
    cpl4[256:512, 128:256] = jnp.where(low, zero, v).astype(BF16)
    offset = pl.multiple_of(t * SLICE, SLICE)
    outer(lambda rows: acts[rows, pl.ds(offset, SLICE)], cpl4, 0)
    send_grad(2)
    send_grad(3)

    ones = jnp.ones((CHUNK, 128), BF16)

    def gather(n):
        pltpu.make_async_copy(sb.at[n, d], rb.at[n, d], own_sem.at[n]).wait()
        wait_bytes(rb.at[n, pl.ds(0, NDP - 1)], rcv.at[2 + n])
        trans[...] = rb[n].reshape(1024, 128).astype(F32)
        for jp in range(8):
            grad[:, jp * 128:(jp + 1) * 128] = trans[pl.ds(jp, 128, stride=8), :].astype(BF16)
        rowsum[...] += dot(grad[...], ones)

    def planes(n, cols, width):
        g = grad[...]
        for q in range(2):
            v = nib[n, q, :, :, cols].reshape(CHUNK, width)
            yield q, 0, dot(g, v)
            for i, k in enumerate((4, 3, 2)):
                shift = jnp.asarray(2.0 ** (7 + k), BF16)
                yield q, i + 1, dot(g, (v + shift) - shift)

    def accumulate(n, _):
        gather(n)
        for q, i, v in planes(n, pl.ds(0, WORDS), WORDS):
            acc[q, i] += v
        return 0

    accumulate(0, 0)
    convert(2)
    accumulate(1, 0)
    convert(3)
    accumulate(2, 0)
    gather(3)

    def compute(s):
        per, base = PER[s], BEFORE[s]
        got = {}
        for q, i, v in planes(3, pl.ds(STARTS[s], WIDTHS[s]), WIDTHS[s]):
            got[q, i] = v
        r = rowsum[...]
        for h in range(per // 8):
            at = slice(STARTS[s] + h * 128, STARTS[s] + (h + 1) * 128)
            for q in range(2):
                d0, d4, d3, d2 = (
                    got[q, i][:, h * 128:(h + 1) * 128] + acc[q, i, :, at] for i in range(4)
                )
                a4, a3 = d4 * 0.125, d3 * 0.25
                p3 = a4 - r
                p2 = a3 - a4 - r
                p1 = d2 * 0.5 - a3 - a4 - r
                p0 = 2.0 * d0 - d2 - 2.0 * a3 - 2.0 * a4 - 1.5 * r
                for i, p in enumerate((p0, p1, p2, p3)):
                    row = base * 128 + h * 8 + q * 4 + i
                    for dd in range(NDP):
                        if AXES[s] == "x":
                            e, step = dd // 2 * 8, 1
                        elif AXES[s] == "z":
                            e, step = dd // 2, 8
                        else:
                            e, step = dd // 2 % 2 * 32 + dd // 4, 4
                        e = e + dd % 2 * 64
                        part[pl.ds(e * per + row, 8, stride=step * per), :] = p[dd * 8:(dd + 1) * 8, :]
        half = 64 * per
        theirs = pl.ds(pl.multiple_of(base * 128 + (1 - core) * half, half), half)
        sent = pl.ds(base * 64, half)
        s0[sent, :] = part[theirs, :].astype(BF16)
        pltpu.make_async_remote_copy(
            src_ref=s0.at[sent],
            dst_ref=r0.at[sent],
            send_sem=snd.at[6 + 3 * s],
            recv_sem=rcv.at[6 + 3 * s],
            device_id={"dp": d + 1 - 2 * core, "tensor": t},
            device_id_type=MESH,
        ).start()

    def along(s):
        per, base = PER[s], BEFORE[s]
        group = 16 * per
        wait_bytes(r0.at[pl.ds(base * 64, 4 * group)], rcv.at[6 + 3 * s])
        a = {"x": x, "y": y_hi * 2 + y_lo, "z": z}[AXES[s]]
        for k in (1, 2, 3, 0):
            g = (a + k) % 4
            if AXES[s] == "y":
                pieces = [
                    (pl.multiple_of(((g % 2) * 4 + i) * 8 * per + (g // 2) * 4 * per, 4 * per), 4 * per)
                    for i in range(4)
                ]
            else:
                pieces = [(pl.multiple_of(g * group, group), group)]
            v = [
                part[pl.ds(pl.multiple_of(base * 128 + core * 4 * group + o, n), n), :]
                + r0[pl.ds(pl.multiple_of(base * 64 + o, n), n), :].astype(F32)
                for o, n in pieces
            ]
            v = v[0] if len(v) == 1 else jnp.concatenate(v, axis=0)
            if k == 0:
                k1[pl.ds(base * 16, group), :] = v
                continue
            sent = pl.ds(base * 48 + (k - 1) * group, group)
            s1[sent, :] = v.astype(BF16)
            if AXES[s] == "x":
                peer = {"dp": g * 4 + d % 4, "tensor": t}
            elif AXES[s] == "z":
                peer = {"dp": d, "tensor": g * 2 + y_hi}
            else:
                peer = {"dp": x * 4 + (g % 2) * 2 + core, "tensor": z * 2 + g // 2}
            pltpu.make_async_remote_copy(
                src_ref=s1.at[sent],
                dst_ref=r1.at[sent],
                send_sem=snd.at[7 + 3 * s],
                recv_sem=rcv.at[7 + 3 * s],
                device_id=peer,
                device_id_type=MESH,
            ).start()

    place = {"x": y_lo * 8 + t, "z": y_hi * 8 + x * 2 + y_lo, "y": z * 4 + x}

    def last_stage(s):
        if PER[s] == 16:
            return s2b, r2b, [i for i in range(NS) if PER[i] == 16].index(s)
        return s2f, r2f, [i for i in range(NS) if PER[i] == 8].index(s)

    def across(s):
        per, base = PER[s], BEFORE[s]
        group = 16 * per
        wait_bytes(r1.at[pl.ds(base * 48, 3 * group)], rcv.at[7 + 3 * s])
        v = k1[pl.ds(base * 16, group), :]
        for k in range(3):
            v = v + r1[pl.ds(base * 48 + k * group, group), :].astype(F32)
        k1[pl.ds(base * 16, group), :] = v
        have, into, n = last_stage(s)
        have[n] = v.reshape(16, per, 128).astype(have.dtype)
        m = place[AXES[s]]

        def one(k, _):
            mm = (m + k) % 16
            if AXES[s] == "x":
                peer = {"dp": x * 4 + (mm // 8) * 2 + core, "tensor": mm % 8}
            elif AXES[s] == "z":
                peer = {"dp": (mm % 8) * 2 + core, "tensor": z * 2 + mm // 8}
            else:
                peer = {"dp": (mm % 4) * 4 + d % 4, "tensor": (mm // 4) * 2 + y_hi}
            pltpu.make_async_remote_copy(
                src_ref=have.at[n, mm],
                dst_ref=into.at[n, k - 1],
                send_sem=snd.at[8 + 3 * s],
                recv_sem=rcv.at[8 + 3 * s],
                device_id=peer,
                device_id_type=MESH,
            ).start()
            return 0

        lax.fori_loop(1, 16, one, 0)

    def owned(s, score):
        per, base = PER[s], BEFORE[s]
        _, into, n = last_stage(s)
        wait_bytes(into.at[n], rcv.at[8 + 3 * s])
        v = k1[pl.ds(pl.multiple_of(base * 16 + place[AXES[s]] * per, per), per), :]
        for k in range(15):
            v = v + into[n, k].astype(F32)
        for h in range(per // 8):
            feat[pl.ds(STARTS[s] // 128 + h, 8, stride=8), :] = v[h * 8:(h + 1) * 8, :]

        def one(b, total):
            for h in range(per // 8):
                row = b * 8 + STARTS[s] // 128 + h
                cols = pl.ds(pl.multiple_of(row * 128, 128), 128)
                total = total + feat[pl.ds(row, 1), :] * bank[:, cols].astype(F32)
            return total

        score = lax.fori_loop(0, 8, one, score)
        return score

    compute(0)
    compute(1)
    compute(2)
    along(0)
    compute(3)
    along(1)
    compute(4)
    along(2)
    along(3)
    along(4)
    c_bank.wait()
    c_vrows.wait()
    for s in range(NS):
        across(s)
    score = jnp.zeros((128, 128), F32)
    for s in range(NS):
        score = owned(s, score)

    f = feat[...]
    mean = jnp.sum(f * f, keepdims=True) * (1.0 / (8 * WORDS))
    inv = lax.rsqrt(mean + 1e-06)
    out[0:64, :] = f * inv
    by_row = jnp.sum(score, axis=1, keepdims=True)
    pick = lax.broadcasted_iota(jnp.int32, (128, 64), 0) == vrows[...]
    chosen = jnp.sum(jnp.where(pick, by_row, 0.0), axis=0, keepdims=True)
    out[64:65, 0:64] = chosen * inv * (1.0 / math.sqrt(8 * WORDS))

    wait_bytes(pu_recv, snd.at[0])
    wait_bytes(cpl_recv.at[pl.ds(0, NT - 1)], snd.at[1])
    for n in range(4):
        wait_bytes(sb.at[n, pl.ds(0, NDP - 1)], snd.at[2 + n])
    for s in range(NS):
        group = 16 * PER[s]
        wait_bytes(s0.at[pl.ds(BEFORE[s] * 64, 4 * group)], snd.at[6 + 3 * s])
        wait_bytes(s1.at[pl.ds(BEFORE[s] * 48, 3 * group)], snd.at[7 + 3 * s])
        have, _, n = last_stage(s)
        wait_bytes(have.at[n, pl.ds(0, 15)], snd.at[8 + 3 * s])


def split(both, feat, score):
    feat[...] = both[0:64, :]
    score[...] = both[64:65, 0:64]


def per_device(acts, og, down, up, counts, signs, bank, vrows):
    anywhere = pl.BlockSpec(memory_space=pl.ANY)
    vmem = pltpu.VMEM
    both = pl.pallas_call(
        body,
        out_shape=jax.ShapeDtypeStruct((72, 128), F32),
        in_specs=[
            anywhere, anywhere, anywhere, anywhere,
            pl.BlockSpec(memory_space=pltpu.SMEM),
            anywhere, anywhere, anywhere,
        ],
        out_specs=pl.BlockSpec(memory_space=pltpu.VMEM),
        scratch_shapes=[
            vmem((EPD * SEQ, WIDTH), BF16),
            vmem((EPD * SEQ, SLICE), BF16),
            vmem((2 * RANK, WIDTH), BF16),
            vmem((2 * RANK, SLICE), BF16),
            vmem((128, 8 * WORDS), BF16),
            vmem((1, 64), jnp.int32),
            vmem((ROWS, 128, WORDS), jnp.int32),
            vmem((4, 2, 8, 128, WORDS), BF16),
            vmem((256, 128), F32),
            vmem((NT - 1, 32, 128), F32),
            vmem((NT, 32, 128), BF16),
            vmem((EPD * SEQ, 256), BF16),
            vmem((EPD * SEQ, 256), BF16),
            vmem((4, NDP, 64, 128), BF16),
            vmem((4, NDP, 64, 128), BF16),
            vmem((1024, 128), F32),
            vmem((128, CHUNK), BF16),
            vmem((2, 4, 128, WORDS), F32),
            vmem((128, 128), F32),
            vmem((128 * 64, 128), F32),
            vmem((64 * 64, 128), BF16),
            vmem((64 * 64, 128), BF16),
            vmem((48 * 64, 128), BF16),
            vmem((48 * 64, 128), BF16),
            vmem((16 * 64, 128), F32),
            vmem((3, 16, 16, 128), BF16),
            vmem((3, 15, 16, 128), BF16),
            vmem((2, 16, 8, 128), F32),
            vmem((2, 15, 8, 128), F32),
            vmem((64, 128), F32),
            pltpu.SemaphoreType.DMA((12,)),
            pltpu.SemaphoreType.DMA((8,)),
            pltpu.SemaphoreType.DMA((4,)),
            pltpu.SemaphoreType.DMA((6 + 3 * NS,)),
            pltpu.SemaphoreType.DMA((6 + 3 * NS,)),
        ],
        compiler_params=pltpu.CompilerParams(
            collective_id=0, has_side_effects=True, vmem_limit_bytes=63 << 20
        ),
    )(
        acts.reshape(EPD * SEQ, WIDTH),
        og.reshape(EPD * SEQ, SLICE),
        down,
        up.T,
        counts,
        signs.reshape(ROWS, 128, WORDS),
        bank,
        vrows.reshape(1, 64),
    )
    feat, score = pl.pallas_call(
        split,
        out_shape=(
            jax.ShapeDtypeStruct((64, 128), F32),
            jax.ShapeDtypeStruct((1, 64), F32),
        ),
    )(both)
    return feat.reshape(1, 8 * WORDS), score


def solution(mesh):
    in_specs = (
        P("dp", None, None),
        P("dp", None, "tensor"),
        P(),
        P("tensor", None),
        P("dp"),
        P("tensor", "dp", None, None),
        P(),
        P(),
    )
    out_specs = (P(("dp", "tensor"), None), P(("dp", "tensor"), None))
    return jax.shard_map(
        per_device, mesh=mesh, in_specs=in_specs, out_specs=out_specs, check_vma=False
    )
```

```python
import math

import jax
import jax.numpy as jnp
from jax import lax
from jax.experimental import pallas as pl
from jax.experimental.pallas import tpu as pltpu
from jax.sharding import PartitionSpec as P

BF16 = jnp.bfloat16
F32 = jnp.float32
MESH = pl.DeviceIdType.MESH

NDP = 16
NT = 8
EPD = 8
SEQ = 64
RANK = 64
WIDTH = 4096
SLICE = 512
ROWS = 32
WORDS = 1024
CHUNK = 1024
PARTS = ((1, 0), (1, 1), (0, 0), (0, 1))
HOPS = (4, 12, 8, 2, 5, 13, 9, 3, 6, 14, 10, 1, 7, 15, 11)
AXES = ("x", "z", "y", "x", "z")
WIDTHS = (256, 256, 256, 128, 128)
NS = len(AXES)
STARTS = tuple(sum(WIDTHS[:s]) for s in range(NS))
PER = tuple(w // 16 for w in WIDTHS)
BEFORE = tuple(w // 16 for w in STARTS)


def dot(a, b, dims=(((1,), (0,)), ((), ()))):
    return lax.dot_general(a, b, dims, preferred_element_type=F32)


def body(
    acts_hbm, og_hbm, down_hbm, up_hbm, counts, signs_hbm, bank_hbm, vrows_hbm,
    out,
    acts, mg, down2, up2, bank, vrows, words, nib,
    pu, pu_recv, cpl_recv, cpl4, hid4,
    sb, rb, trans, grad, acc, rowsum,
    part, s0, r0, s1, r1, k1, s2b, r2b, s2f, r2f, feat,
    in_sem, word_sem, own_sem, snd, rcv,
):
    d = lax.axis_index("dp")
    t = lax.axis_index("tensor")
    x = d // 4
    y_lo = (d // 2) % 2
    core = d % 2
    z = t // 2
    y_hi = t % 2

    def load(src, dst, n):
        c = pltpu.make_async_copy(src, dst, in_sem.at[n])
        c.start()
        return c

    c_og = load(og_hbm, mg, 0)
    c_up = [load(up_hbm, up2.at[pl.ds(i * RANK, RANK)], 10 + i) for i in range(2)]
    c_down = [load(down_hbm, down2.at[pl.ds(i * RANK, RANK)], 2 + i) for i in range(2)]
    for i in range(4):
        load(acts_hbm.at[pl.ds(i * 128, 128)], acts.at[pl.ds(i * 128, 128)], 4 + i)

    barrier = pltpu.get_barrier_semaphore()

    def greet(dd, tt):
        pl.semaphore_signal(
            barrier, inc=1, device_id={"dp": dd, "tensor": tt}, device_id_type=MESH
        )

    for k in range(1, NDP):
        greet((d + k) % NDP, t)
    for k in range(1, NT):
        greet(d, (t + k) % NT)
    d_flip = d + 2 - 4 * y_lo
    t_flip = t + 1 - 2 * y_hi
    for k in range(1, NT):
        greet(d_flip, (t + k) % NT)
    for k in range(1, 8):
        m = (x * 2 + y_lo + k) % 8
        greet(m * 2 + core, t_flip)
    for k in range(1, 4):
        for i in range(1, 4):
            greet((d + 4 * k) % NDP, (t + 2 * i) % NT)

    lane = lax.broadcasted_iota(jnp.int32, (1, 128), 1)
    low = lane < 64

    def split4(v):
        zero = jnp.zeros_like(v)
        return jnp.concatenate([jnp.where(low, v, zero), jnp.where(low, zero, v)], axis=1)

    c_og.wait()
    token = lax.broadcasted_iota(jnp.int32, (SEQ, SLICE), 0)
    for e in range(EPD):
        rows = pl.ds(e * SEQ, SEQ)
        v = mg[rows, :].astype(F32)
        mg[rows, :] = jnp.where(token < counts[e], v, 0.0).astype(BF16)

    for c in c_up:
        c.wait()
    u = dot(mg[...], up2[...], (((1,), (1,)), ((), ())))
    pu[...] = jnp.where(low, u[0:256, :], u[256:512, :])

    pl.semaphore_wait(barrier, 45)

    def send_pu(k, _):
        tt = (t + k) % NT
        pltpu.make_async_remote_copy(
            src_ref=pu.at[pl.ds(pl.multiple_of(tt * 32, 32), 32)],
            dst_ref=pu_recv.at[k - 1],
            send_sem=snd.at[0],
            recv_sem=rcv.at[0],
            device_id={"dp": d, "tensor": tt},
            device_id_type=MESH,
        ).start()
        return 0

    lax.fori_loop(1, NT, send_pu, 0)

    for c in c_down:
        c.wait()
    def hidden(i, _):
        rows = pl.ds(pl.multiple_of(i * 128, 128), 128)
        pltpu.make_async_copy(acts_hbm.at[rows], acts.at[rows], in_sem.at[4 + i]).wait()
        h = dot(acts[rows, :], down2[...], (((1,), (1,)), ((), ())))
        hid4[rows, :] = split4(h).astype(BF16)
        return 0

    lax.fori_loop(0, 2, hidden, 0)
    c_words = []
    for n, (half, c) in enumerate(PARTS):
        for hi in range(2):
            at = pl.ds(16 * hi + 8 * c, 8), pl.ds(half * RANK, RANK)
            copy = pltpu.make_async_copy(signs_hbm.at[at], words.at[at], word_sem.at[2 * n + hi])
            copy.start()
            c_words.append(copy)
    c_bank = load(bank_hbm, bank, 8)
    c_vrows = load(vrows_hbm, vrows, 9)
    acc[...] = jnp.zeros_like(acc)
    rowsum[...] = jnp.zeros_like(rowsum)
    lax.fori_loop(2, 4, hidden, 0)

    def outer(lhs, rhs, half):
        def product(e):
            rows = pl.ds(pl.multiple_of(e * SEQ, SEQ), SEQ)
            o = dot(lhs(rows), rhs[rows, :], (((0,), (0,)), ((), ())))
            o = o.reshape(NDP, 2, 16, 256)
            return o[:, 0, :, 0:128] + o[:, 1, :, 128:256]

        def one(p, _):
            g0, g1 = product(2 * p), product(2 * p + 1)
            for c in range(2):
                g = jnp.concatenate([g0[:, c * 8:c * 8 + 8], g1[:, c * 8:c * 8 + 8]], axis=1)
                sb[2 * (1 - half) + c, :, pl.ds(pl.multiple_of(p * 16, 16), 16), :] = g.astype(BF16)
            return 0

        lax.fori_loop(0, EPD // 2, one, 0, unroll=True)

    def send_grad(n):
        for k in HOPS:
            dd = (d + k) % NDP
            pltpu.make_async_remote_copy(
                src_ref=sb.at[n, dd],
                dst_ref=rb.at[n, d],
                send_sem=snd.at[2 + n],
                recv_sem=rcv.at[2 + n],
                device_id={"dp": dd, "tensor": t},
                device_id_type=MESH,
            ).start()
        pltpu.make_async_copy(sb.at[n, d], rb.at[n, d], own_sem.at[n]).start()

    def wait_bytes(ref, sem):
        pltpu.make_async_copy(ref, ref, sem).wait()

    outer(lambda rows: mg[rows, :], hid4, 1)

    wait_bytes(pu_recv, rcv.at[0])
    total = pu[pl.ds(pl.multiple_of(t * 32, 32), 32), :]
    for k in range(NT - 1):
        total = total + pu_recv[k]
    cpl_recv[t] = total.astype(BF16)

    def send_cpl(k, _):
        tt = (t + k) % NT
        pltpu.make_async_remote_copy(
            src_ref=cpl_recv.at[t],
            dst_ref=cpl_recv.at[t],
            send_sem=snd.at[1],
            recv_sem=rcv.at[1],
            device_id={"dp": d, "tensor": tt},
            device_id_type=MESH,
        ).start()
        return 0

    lax.fori_loop(1, NT, send_cpl, 0)
    send_grad(0)
    send_grad(1)

    def convert(n):
        half, c = PARTS[n]
        quarter = jnp.asarray(0.25, BF16)
        for hi in range(2):
            c_words[2 * n + hi].wait()

            def one(k, _):
                w = words[8 * c + k + 16 * hi, pl.ds(half * RANK, RANK), :]
                rows = pl.ds(hi * RANK, RANK)
                nib[n, 0, k, rows, :] = (w & 15).astype(F32).astype(BF16) + quarter
                nib[n, 1, k, rows, :] = (w >> 4).astype(F32).astype(BF16) + quarter
                return 0

            lax.fori_loop(0, 8, one, 0)

    convert(0)
    convert(1)
    convert(2)

    wait_bytes(cpl_recv.at[pl.ds(0, NT - 1)], rcv.at[1])
    v = cpl_recv[...].reshape(256, 128).astype(F32)
    w = pltpu.roll(v, 64, 1)
    zero = jnp.zeros_like(v)
    cpl4[0:256, 0:128] = jnp.where(low, v, zero).astype(BF16)
    cpl4[0:256, 128:256] = jnp.where(low, zero, w).astype(BF16)
    cpl4[256:512, 0:128] = jnp.where(low, w, zero).astype(BF16)
    cpl4[256:512, 128:256] = jnp.where(low, zero, v).astype(BF16)
    offset = pl.multiple_of(t * SLICE, SLICE)
    outer(lambda rows: acts[rows, pl.ds(offset, SLICE)], cpl4, 0)
    send_grad(2)
    send_grad(3)

    ones = jnp.ones((CHUNK, 128), BF16)

    def gather(n, at):
        pltpu.make_async_copy(sb.at[n, d], rb.at[n, d], own_sem.at[n]).wait()
        wait_bytes(rb.at[n, pl.ds(0, NDP - 1)], rcv.at[2 + n])
        trans[...] = rb[n].reshape(1024, 128).astype(F32)
        for jp in range(8):
            cols = slice(at + jp * 128, at + (jp + 1) * 128)
            grad[:, cols] = trans[pl.ds(jp, 128, stride=8), :].astype(BF16)
        rowsum[...] += dot(grad[:, at:at + CHUNK], ones)

    def planes(g, v):
        for q in range(2):
            n = v(q)
            n = n.reshape(-1, n.shape[-1])
            yield q, 0, dot(g, n)
            for i, k in enumerate((4, 3, 2)):
                shift = jnp.asarray(2.0 ** (7 + k), BF16)
                yield q, i + 1, dot(g, (n + shift) - shift)

    def accumulate(n, _):
        gather(n, 0)
        for q, i, v in planes(grad[:, 0:CHUNK], lambda q: nib[n, q]):
            acc[q, i] += v
        return 0

    lax.fori_loop(0, 2, accumulate, 0)
    convert(3)
    gather(2, 0)
    gather(3, CHUNK)

    def compute(s):
        per, base = PER[s], BEFORE[s]
        got = {}
        for q, i, v in planes(grad[...], lambda q: nib[2:4, q, :, :, pl.ds(STARTS[s], WIDTHS[s])]):
            got[q, i] = v
        r = rowsum[...]
        for h in range(per // 8):
            at = slice(STARTS[s] + h * 128, STARTS[s] + (h + 1) * 128)
            for q in range(2):
                d0, d4, d3, d2 = (
                    got[q, i][:, h * 128:(h + 1) * 128] + acc[q, i, :, at] for i in range(4)
                )
                a4, a3 = d4 * 0.125, d3 * 0.25
                p3 = a4 - r
                p2 = a3 - a4 - r
                p1 = d2 * 0.5 - a3 - a4 - r
                p0 = 2.0 * d0 - d2 - 2.0 * a3 - 2.0 * a4 - 1.5 * r
                for i, p in enumerate((p0, p1, p2, p3)):
                    row = base * 128 + h * 8 + q * 4 + i
                    for dd in range(NDP):
                        if AXES[s] == "x":
                            e, step = dd // 2 * 8, 1
                        elif AXES[s] == "z":
                            e, step = dd // 2, 8
                        else:
                            e, step = dd // 2 % 2 * 32 + dd // 4, 4
                        e = e + dd % 2 * 64
                        part[pl.ds(e * per + row, 8, stride=step * per), :] = p[dd * 8:(dd + 1) * 8, :]
        half = 64 * per
        theirs = pl.ds(pl.multiple_of(base * 128 + (1 - core) * half, half), half)
        sent = pl.ds(base * 64, half)
        s0[sent, :] = part[theirs, :].astype(BF16)
        pltpu.make_async_remote_copy(
            src_ref=s0.at[sent],
            dst_ref=r0.at[sent],
            send_sem=snd.at[6 + 3 * s],
            recv_sem=rcv.at[6 + 3 * s],
            device_id={"dp": d + 1 - 2 * core, "tensor": t},
            device_id_type=MESH,
        ).start()

    def along(s):
        per, base = PER[s], BEFORE[s]
        group = 16 * per
        wait_bytes(r0.at[pl.ds(base * 64, 4 * group)], rcv.at[6 + 3 * s])
        a = {"x": x, "y": y_hi * 2 + y_lo, "z": z}[AXES[s]]
        for k in (1, 2, 3, 0):
            g = (a + k) % 4
            if AXES[s] == "y":
                pieces = [
                    (pl.multiple_of(((g % 2) * 4 + i) * 8 * per + (g // 2) * 4 * per, 4 * per), 4 * per)
                    for i in range(4)
                ]
            else:
                pieces = [(pl.multiple_of(g * group, group), group)]
            v = [
                part[pl.ds(pl.multiple_of(base * 128 + core * 4 * group + o, n), n), :]
                + r0[pl.ds(pl.multiple_of(base * 64 + o, n), n), :].astype(F32)
                for o, n in pieces
            ]
            v = v[0] if len(v) == 1 else jnp.concatenate(v, axis=0)
            if k == 0:
                k1[pl.ds(base * 16, group), :] = v
                continue
            sent = pl.ds(base * 48 + (k - 1) * group, group)
            s1[sent, :] = v.astype(BF16)
            if AXES[s] == "x":
                peer = {"dp": g * 4 + d % 4, "tensor": t}
            elif AXES[s] == "z":
                peer = {"dp": d, "tensor": g * 2 + y_hi}
            else:
                peer = {"dp": x * 4 + (g % 2) * 2 + core, "tensor": z * 2 + g // 2}
            pltpu.make_async_remote_copy(
                src_ref=s1.at[sent],
                dst_ref=r1.at[sent],
                send_sem=snd.at[7 + 3 * s],
                recv_sem=rcv.at[7 + 3 * s],
                device_id=peer,
                device_id_type=MESH,
            ).start()

    place = {"x": y_lo * 8 + t, "z": y_hi * 8 + x * 2 + y_lo, "y": z * 4 + x}

    def last_stage(s):
        if PER[s] == 16:
            return s2b, r2b, [i for i in range(NS) if PER[i] == 16].index(s)
        return s2f, r2f, [i for i in range(NS) if PER[i] == 8].index(s)

    def across(s):
        per, base = PER[s], BEFORE[s]
        group = 16 * per
        wait_bytes(r1.at[pl.ds(base * 48, 3 * group)], rcv.at[7 + 3 * s])
        v = k1[pl.ds(base * 16, group), :]
        for k in range(3):
            v = v + r1[pl.ds(base * 48 + k * group, group), :].astype(F32)
        k1[pl.ds(base * 16, group), :] = v
        have, into, n = last_stage(s)
        have[n] = v.reshape(16, per, 128).astype(have.dtype)
        m = place[AXES[s]]

        def one(k, _):
            mm = (m + k) % 16
            if AXES[s] == "x":
                peer = {"dp": x * 4 + (mm // 8) * 2 + core, "tensor": mm % 8}
            elif AXES[s] == "z":
                peer = {"dp": (mm % 8) * 2 + core, "tensor": z * 2 + mm // 8}
            else:
                peer = {"dp": (mm % 4) * 4 + d % 4, "tensor": (mm // 4) * 2 + y_hi}
            pltpu.make_async_remote_copy(
                src_ref=have.at[n, mm],
                dst_ref=into.at[n, k - 1],
                send_sem=snd.at[8 + 3 * s],
                recv_sem=rcv.at[8 + 3 * s],
                device_id=peer,
                device_id_type=MESH,
            ).start()
            return 0

        lax.fori_loop(1, 16, one, 0, unroll=True)

    def owned(s, score):
        per, base = PER[s], BEFORE[s]
        _, into, n = last_stage(s)
        wait_bytes(into.at[n], rcv.at[8 + 3 * s])
        v = k1[pl.ds(pl.multiple_of(base * 16 + place[AXES[s]] * per, per), per), :]
        for k in range(15):
            v = v + into[n, k].astype(F32)
        for h in range(per // 8):
            feat[pl.ds(STARTS[s] // 128 + h, 8, stride=8), :] = v[h * 8:(h + 1) * 8, :]

        def one(b, total):
            for h in range(per // 8):
                row = b * 8 + STARTS[s] // 128 + h
                cols = pl.ds(pl.multiple_of(row * 128, 128), 128)
                total = total + feat[pl.ds(row, 1), :] * bank[:, cols].astype(F32)
            return total

        score = lax.fori_loop(0, 8, one, score, unroll=True)
        return score

    compute(0)
    compute(1)
    compute(2)
    along(0)
    compute(3)
    along(1)
    compute(4)
    along(2)
    along(3)
    along(4)
    c_bank.wait()
    c_vrows.wait()
    score = jnp.zeros((128, 128), F32)
    across(0)
    across(1)
    across(2)
    across(3)
    across(4)
    for s in range(NS):
        score = owned(s, score)

    f = feat[...]
    mean = jnp.sum(f * f, keepdims=True) * (1.0 / (8 * WORDS))
    inv = lax.rsqrt(mean + 1e-06)
    out[0:64, :] = f * inv
    by_row = jnp.sum(score, axis=1, keepdims=True)
    pick = lax.broadcasted_iota(jnp.int32, (128, 64), 0) == vrows[...]
    chosen = jnp.sum(jnp.where(pick, by_row, 0.0), axis=0, keepdims=True)
    out[64:65, 0:64] = chosen * inv * (1.0 / math.sqrt(8 * WORDS))

    wait_bytes(pu_recv, snd.at[0])
    wait_bytes(cpl_recv.at[pl.ds(0, NT - 1)], snd.at[1])
    for n in range(4):
        wait_bytes(sb.at[n, pl.ds(0, NDP - 1)], snd.at[2 + n])
    for s in range(NS):
        group = 16 * PER[s]
        wait_bytes(s0.at[pl.ds(BEFORE[s] * 64, 4 * group)], snd.at[6 + 3 * s])
        wait_bytes(s1.at[pl.ds(BEFORE[s] * 48, 3 * group)], snd.at[7 + 3 * s])
        have, _, n = last_stage(s)
        wait_bytes(have.at[n, pl.ds(0, 15)], snd.at[8 + 3 * s])


def split(both, feat, score):
    feat[...] = both[0:64, :]
    score[...] = both[64:65, 0:64]


def per_device(acts, og, down, up, counts, signs, bank, vrows):
    anywhere = pl.BlockSpec(memory_space=pl.ANY)
    vmem = pltpu.VMEM
    both = pl.pallas_call(
        body,
        out_shape=jax.ShapeDtypeStruct((72, 128), F32),
        in_specs=[
            anywhere, anywhere, anywhere, anywhere,
            pl.BlockSpec(memory_space=pltpu.SMEM),
            anywhere, anywhere, anywhere,
        ],
        out_specs=pl.BlockSpec(memory_space=pltpu.VMEM),
        scratch_shapes=[
            vmem((EPD * SEQ, WIDTH), BF16),
            vmem((EPD * SEQ, SLICE), BF16),
            vmem((2 * RANK, WIDTH), BF16),
            vmem((2 * RANK, SLICE), BF16),
            vmem((128, 8 * WORDS), BF16),
            vmem((1, 64), jnp.int32),
            vmem((ROWS, 128, WORDS), jnp.int32),
            vmem((4, 2, 8, 128, WORDS), BF16),
            vmem((256, 128), F32),
            vmem((NT - 1, 32, 128), F32),
            vmem((NT, 32, 128), BF16),
            vmem((EPD * SEQ, 256), BF16),
            vmem((EPD * SEQ, 256), BF16),
            vmem((4, NDP, 64, 128), BF16),
            vmem((4, NDP, 64, 128), BF16),
            vmem((1024, 128), F32),
            vmem((128, 2 * CHUNK), BF16),
            vmem((2, 4, 128, WORDS), F32),
            vmem((128, 128), F32),
            vmem((128 * 64, 128), F32),
            vmem((64 * 64, 128), BF16),
            vmem((64 * 64, 128), BF16),
            vmem((48 * 64, 128), BF16),
            vmem((48 * 64, 128), BF16),
            vmem((16 * 64, 128), F32),
            vmem((3, 16, 16, 128), BF16),
            vmem((3, 15, 16, 128), BF16),
            vmem((2, 16, 8, 128), F32),
            vmem((2, 15, 8, 128), F32),
            vmem((64, 128), F32),
            pltpu.SemaphoreType.DMA((12,)),
            pltpu.SemaphoreType.DMA((8,)),
            pltpu.SemaphoreType.DMA((4,)),
            pltpu.SemaphoreType.DMA((6 + 3 * NS,)),
            pltpu.SemaphoreType.DMA((6 + 3 * NS,)),
        ],
        compiler_params=pltpu.CompilerParams(
            collective_id=0, has_side_effects=True, vmem_limit_bytes=63 << 20
        ),
    )(
        acts.reshape(EPD * SEQ, WIDTH),
        og.reshape(EPD * SEQ, SLICE),
        down,
        up.T,
        counts,
        signs.reshape(ROWS, 128, WORDS),
        bank,
        vrows.reshape(1, 64),
    )
    feat, score = pl.pallas_call(
        split,
        out_shape=(
            jax.ShapeDtypeStruct((64, 128), F32),
            jax.ShapeDtypeStruct((1, 64), F32),
        ),
    )(both)
    return feat.reshape(1, 8 * WORDS), score


def solution(mesh):
    in_specs = (
        P("dp", None, None),
        P("dp", None, "tensor"),
        P(),
        P("tensor", None),
        P("dp"),
        P("tensor", "dp", None, None),
        P(),
        P(),
    )
    out_specs = (P(("dp", "tensor"), None), P(("dp", "tensor"), None))
    return jax.shard_map(
        per_device, mesh=mesh, in_specs=in_specs, out_specs=out_specs, check_vma=False
    )
```
